32 devices in a mesh: seg: 8 (over y, x, core), tok: 4 (over z).
Axes of the slice: x: 2, y: 2, z: 4, core: 2. Of those that a mesh axis runs over, the one named last changes fastest.
Arguments:
- value: bfloat16 [524288, 128], P(('seg', 'tok')), may hold values from -6 to 6
- gate_in: bfloat16 [524288, 128], P(('seg', 'tok')), may hold values from -6 to 6
- gate_out: bfloat16 [524288, 128], P(('seg', 'tok')), may hold values from -6 to 6
- filter_spectrum: bfloat16 [2, 256, 512, 128], P(None, 'tok'), may hold values from -8 to 8, as said below
- skip_gain: float32 [128], replicated, may hold values from 0.25 to 2
Outputs:
- mixed_out: bfloat16 [524288, 128], P(('seg', 'tok'))
The draws below stay inside these ranges and needn't reach their ends.
Inputs may be any that keep to these rules, and one draw needn't show every extreme that they name: `filter_spectrum`: the response of a real filter whose taps beyond the first 65536 are zero, rounded.
All inputs are finite; a program needn't handle non-finite values.
Results may differ from the reference program's by a relative error of at most 0.0085.
Values may be sent and summed in bfloat16 or wider, within the bound.
A program may use at most 192 MiB of HBM per device.

```python
import math
import jax
import jax.numpy as jnp
from jax import lax

SEG = 65536
N1 = 256
N2 = 512
CH = 128
TOKENS = 524288
N_SEG = 8


def angle_tables(row_count, col_count, modulus):
    rows = jnp.arange(row_count, dtype=jnp.int32)
    cols = jnp.arange(col_count, dtype=jnp.int32)
    product = rows[:, None] * cols[None, :] % modulus
    angle = product.astype(jnp.float32) * jnp.float32(2.0 * math.pi / modulus)
    return (jnp.cos(angle), jnp.sin(angle))


def draw_filter_spectrum(key, part):
    taps_key, rate_key = jax.random.split(jax.random.fold_in(key, 7))
    rates = jnp.exp(jax.random.uniform(rate_key, (CH,), jnp.float32, math.log(0.25), math.log(400.0))) / SEG
    position = jnp.arange(SEG, dtype=jnp.float32)
    envelope = jnp.exp(-position[:, None] * rates[None, :]) * jnp.sqrt(1.0 - jnp.exp(-2.0 * rates))[None, :]
    noise = jax.random.normal(taps_key, (SEG, CH), jnp.float32)
    taps = (noise * envelope).reshape(N1 // 2, N2, CH)
    cos_one, sin_one = angle_tables(N1, N1 // 2, N1)
    high = lax.Precision.HIGHEST
    a_real = jnp.einsum('kj,jnc->knc', cos_one, taps, precision=high)
    a_imag = -jnp.einsum('kj,jnc->knc', sin_one, taps, precision=high)
    tw_cos, tw_sin = angle_tables(N1, N2, 2 * SEG)
    tw_cos = tw_cos[:, :, None]
    tw_sin = tw_sin[:, :, None]
    b_real = a_real * tw_cos + a_imag * tw_sin
    b_imag = a_imag * tw_cos - a_real * tw_sin
    cos_two, sin_two = angle_tables(N2, N2, N2)
    x_real = jnp.einsum('knc,nm->kmc', b_real, cos_two, precision=high) + jnp.einsum('knc,nm->kmc', b_imag, sin_two, precision=high)
    x_imag = jnp.einsum('knc,nm->kmc', b_imag, cos_two, precision=high) - jnp.einsum('knc,nm->kmc', b_real, sin_two, precision=high)
    both = jnp.stack([x_real, x_imag])
    return jnp.clip(both, -8.0, 8.0).astype(jnp.bfloat16)


def block_scale(key, extent, cuts, low, high):
    factor_of = 1.0
    for axis_at, parts in cuts:
        steps = jax.random.uniform(jax.random.fold_in(jax.random.fold_in(key, 6), axis_at), (parts,), jnp.float32, low / len(cuts), high / len(cuts))
        factor_of = factor_of * jnp.repeat(jnp.exp(steps), extent[axis_at] // parts).reshape((-1,) + (1,) * (len(extent) - 1 - axis_at))
    return factor_of


def normal_values(stream_key, shape, deviation, limit, cuts=(), kind=jnp.bfloat16):
    values = deviation * jax.random.normal(stream_key, shape, jnp.float32)
    if cuts:
        values = values * block_scale(stream_key, shape, cuts, -0.22, 0.18)
    return jnp.clip(values, -limit, limit).astype(kind)


def setup_inputs(seed: int = 0) -> dict:
    key_list = jax.random.split(jax.random.key(seed), 6)
    value = normal_values(key_list[0], (TOKENS, CH), 1.0, 6.0, ((0, 32),))
    gate_in = normal_values(key_list[1], (TOKENS, CH), 1.0, 6.0, ((0, 32),))
    gate_out = normal_values(key_list[2], (TOKENS, CH), 1.0, 6.0, ((0, 32),))
    filter_spectrum = draw_filter_spectrum(jax.random.fold_in(key_list[5], 71), 0)
    skip_gain = jnp.clip(jnp.exp(jax.random.uniform(key_list[4], (CH,), jnp.float32, math.log(0.25), math.log(2.0))), 0.25, 2.0)
    return dict(value=value, gate_in=gate_in, gate_out=gate_out, filter_spectrum=filter_spectrum, skip_gain=skip_gain)


def span_ids(count):
    return jnp.arange(count, dtype=jnp.int32)


def trig_tables(row_ids, col_ids, modulus):
    product = (row_ids[:, None] * col_ids[None, :]) % modulus
    angle = product.astype(jnp.float32) * jnp.float32(2.0 * math.pi / modulus)
    return jnp.cos(angle), jnp.sin(angle)


def einsum_rows(data, table):
    return jnp.einsum("jnc,nk->jkc", data.astype(jnp.float32), table.astype(jnp.float32))


def reference(value, gate_in, gate_out, filter_spectrum, skip_gain):
    gated = (value.astype(jnp.float32) * gate_in.astype(jnp.float32)).astype(jnp.bfloat16)
    fft_len = N1 * N2
    half_rows = N1 // 2
    cos_one, sin_one = trig_tables(span_ids(N1), span_ids(half_rows), N1)
    cos_one_b = cos_one.astype(jnp.bfloat16)
    nsin_one_b = (-sin_one).astype(jnp.bfloat16)
    cos_two, sin_two = trig_tables(span_ids(N2), span_ids(N2), N2)
    cos_two_b = cos_two.astype(jnp.bfloat16)
    sin_two_b = sin_two.astype(jnp.bfloat16)
    inv_cos, inv_sin = trig_tables(span_ids(N1), span_ids(N1), N1)
    inv_cos_b = inv_cos.astype(jnp.bfloat16)
    inv_nsin_b = (-inv_sin).astype(jnp.bfloat16)
    tw_cos, tw_sin = trig_tables(span_ids(N1), span_ids(N2), fft_len)
    tw_cos = tw_cos[:, :, None]
    tw_sin = tw_sin[:, :, None]
    h_real = filter_spectrum[0].astype(jnp.float32)
    h_imag = filter_spectrum[1].astype(jnp.float32)
    scale = jnp.float32(1.0 / fft_len)

    def one_segment(segment):
        flat = segment.reshape(half_rows, N2 * CH)
        a_real = jnp.dot(cos_one_b, flat, preferred_element_type=jnp.float32).reshape(N1, N2, CH)
        a_imag = jnp.dot(nsin_one_b, flat, preferred_element_type=jnp.float32).reshape(N1, N2, CH)
        b_real = (a_real * tw_cos + a_imag * tw_sin).astype(jnp.bfloat16)
        b_imag = (a_imag * tw_cos - a_real * tw_sin).astype(jnp.bfloat16)
        x_real = einsum_rows(b_real, cos_two_b) + einsum_rows(b_imag, sin_two_b)
        x_imag = einsum_rows(b_imag, cos_two_b) - einsum_rows(b_real, sin_two_b)
        z_real = (x_real * h_real - x_imag * h_imag).astype(jnp.bfloat16)
        z_imag = (x_real * h_imag + x_imag * h_real).astype(jnp.bfloat16)
        p_real = einsum_rows(z_real, cos_two_b) - einsum_rows(z_imag, sin_two_b)
        p_imag = einsum_rows(z_imag, cos_two_b) + einsum_rows(z_real, sin_two_b)
        q_real = (p_real * tw_cos - p_imag * tw_sin).astype(jnp.bfloat16)
        q_imag = (p_imag * tw_cos + p_real * tw_sin).astype(jnp.bfloat16)
        total = jnp.dot(inv_cos_b, q_real.reshape(N1, N2 * CH), preferred_element_type=jnp.float32)
        total = total + jnp.dot(inv_nsin_b, q_imag.reshape(N1, N2 * CH), preferred_element_type=jnp.float32)
        return (total * scale).astype(jnp.bfloat16).reshape(fft_len, CH)

    segments = gated.reshape(N_SEG, half_rows, N2, CH)
    convs = lax.map(one_segment, segments)
    main_part = convs[:, :SEG]
    tail_part = convs[:, SEG:]
    carried = jnp.concatenate([jnp.zeros((1, SEG, CH), jnp.bfloat16), tail_part[:-1]], axis=0)
    mixed = (main_part.astype(jnp.float32) + carried.astype(jnp.float32)).astype(jnp.bfloat16)
    mixed = mixed.reshape(TOKENS, CH)
    result = gate_out.astype(jnp.float32) * (mixed.astype(jnp.float32) + skip_gain[None, :] * gated.astype(jnp.float32))
    return result.astype(jnp.bfloat16)
```

```python
import math

import jax
import jax.numpy as jnp
from jax import lax
from jax.experimental import pallas as pl
from jax.experimental.pallas import tpu as pltpu
from jax.sharding import PartitionSpec as P

N1 = 256
N2 = 512
HALF = N1 // 2
ROWS = HALF + 16
CHUNKS = 2


def span_ids(count):
    return jnp.arange(count, dtype=jnp.int32)


def trig_tables(row_ids, col_ids, modulus):
    product = row_ids[:, None] * col_ids[None, :] % modulus
    angle = product.astype(jnp.float32) * jnp.float32(2.0 * math.pi / modulus)
    return (jnp.cos(angle), jnp.sin(angle))


def half_tables(base):
    rows = span_ids(ROWS)
    k1 = (base + rows) % N1
    used = rows <= HALF
    weight = jnp.where(used, jnp.where((rows == 0) | (rows == HALF), 1.0, 2.0), 0.0)
    weight = weight.astype(jnp.float32) / (N1 * N2)
    cos_one, sin_one = trig_tables(k1, span_ids(HALF), N1)
    forward = jnp.concatenate([cos_one, -sin_one], axis=0).astype(jnp.bfloat16)
    tw = jnp.stack(trig_tables(k1, span_ids(N2), N1 * N2))
    cos_two, sin_two = trig_tables(span_ids(N2), span_ids(N2), N2)
    cos_two = cos_two.astype(jnp.bfloat16)
    sin_two = sin_two.astype(jnp.bfloat16)
    there = jnp.block([[cos_two, -sin_two], [sin_two, cos_two]])
    back = jnp.block([[cos_two, sin_two], [-sin_two, cos_two]])
    inv_cos, inv_sin = trig_tables(span_ids(N1), k1, N1)
    inv_cos = inv_cos.astype(jnp.bfloat16).astype(jnp.float32) * weight[None, :]
    inv_sin = inv_sin.astype(jnp.bfloat16).astype(jnp.float32) * weight[None, :]
    inverse = jnp.concatenate([inv_cos, -inv_sin], axis=1).astype(jnp.bfloat16)
    return forward, tw, there, back, inverse


def conv_kernel(x_ref, h_ref, fwd_ref, tw_ref, there_ref, back_ref, inv_ref, main_ref, tail_ref):
    f32 = jnp.float32
    data = x_ref[:, 0].astype(f32).reshape(HALF, N2).astype(jnp.bfloat16)
    a = jnp.dot(fwd_ref[...], data, preferred_element_type=f32)
    a_re, a_im = a[:ROWS], a[ROWS:]
    tc, ts = tw_ref[0], tw_ref[1]
    b_re = (a_re * tc + a_im * ts).astype(jnp.bfloat16)
    b_im = (a_im * tc - a_re * ts).astype(jnp.bfloat16)
    spec = jnp.dot(
        jnp.concatenate([b_re, b_im], axis=1), there_ref[...], preferred_element_type=f32
    )
    s_re, s_im = spec[:, :N2], spec[:, N2:]
    h_re = h_ref[0, 0].astype(f32)
    h_im = h_ref[0, 1].astype(f32)
    z_re = (s_re * h_re - s_im * h_im).astype(jnp.bfloat16)
    z_im = (s_re * h_im + s_im * h_re).astype(jnp.bfloat16)
    p = jnp.dot(jnp.concatenate([z_re, z_im], axis=1), back_ref[...], preferred_element_type=f32)
    p_re, p_im = p[:, :N2], p[:, N2:]
    q_re = (p_re * tc - p_im * ts).astype(jnp.bfloat16)
    q_im = (p_im * tc + p_re * ts).astype(jnp.bfloat16)
    conv = jnp.dot(inv_ref[...], jnp.concatenate([q_re, q_im], axis=0), preferred_element_type=f32)
    shape = main_ref.shape
    main_ref[...] = conv[:HALF].reshape(shape).astype(jnp.bfloat16)
    tail_ref[...] = conv[HALF:].reshape(shape).astype(jnp.bfloat16)


def conv_call(x, h, tables):
    parts, count, rows, _ = x.shape
    block = pl.BlockSpec((parts, 1, rows, N2), lambda c: (0, c, 0, 0))
    whole = lambda t: pl.BlockSpec(t.shape, lambda c: (0,) * t.ndim)
    out = jax.ShapeDtypeStruct(x.shape, jnp.bfloat16)
    flops = 4 * count * ROWS * N2 * (HALF + 2 * N2 + 2 * N2 + N1)
    return pl.pallas_call(
        conv_kernel,
        grid=(count,),
        in_specs=[block, pl.BlockSpec((1, 2, ROWS, N2), lambda c: (c, 0, 0, 0))]
        + [whole(t) for t in tables],
        out_specs=[block, block],
        out_shape=[out, out],
        compiler_params=pltpu.CompilerParams(vmem_limit_bytes=48 * 1024 * 1024),
        cost_estimate=pl.CostEstimate(
            flops=flops, bytes_accessed=6 * x.size + 2 * h.size, transcendentals=0
        ),
    )(x, h, *tables)


def half_filter(filt, narrow):
    toks, segs = lax.axis_size("tok"), lax.axis_size("seg")
    tok, seg = lax.axis_index("tok"), lax.axis_index("seg")
    rows = filt.shape[1]
    channels = filt.shape[3]
    share = rows // segs
    side = toks // 2
    upper = tok // side
    mine = lax.dynamic_slice(
        filt, (0, seg * share, 0, upper * (channels // 2)), (2, share, N2, channels // 2)
    )
    mine = jnp.transpose(mine, (3, 0, 1, 2)).reshape(side, narrow, 2, share, N2)
    groups = [list(range(side)), list(range(side, toks))]
    mine = lax.all_to_all(mine, "tok", 0, 0, axis_index_groups=groups, tiled=True)
    both = lax.all_gather(mine, "seg")
    both = jnp.transpose(both, (2, 3, 1, 0, 4, 5)).reshape(narrow, 2, HALF, N2)
    first = jnp.transpose(filt[:, 0], (2, 0, 1)).reshape(toks, narrow, 2, N2)
    first = lax.all_to_all(first, "tok", 0, 0, tiled=True)
    last = lax.dynamic_index_in_dim(first, (1 - upper) * side, 0, keepdims=False)
    last = jnp.pad(last[:, :, None], ((0, 0), (0, 0), (0, ROWS - HALF - 1), (0, 0)))
    return jnp.concatenate([both, last], axis=2)


def shards(value, gate_in, gate_out, filter_spectrum, skip_gain):
    f32 = jnp.float32
    toks, segs = lax.axis_size("tok"), lax.axis_size("seg")
    gated = (value.astype(f32) * gate_in.astype(f32)).astype(jnp.bfloat16)
    tokens, channels = gated.shape
    narrow = channels // toks
    rows = tokens // N2
    step = narrow // CHUNKS
    upper = lax.axis_index("tok") // (toks // 2)
    tables = half_tables(upper * HALF)
    turned = jnp.transpose(gated.reshape(rows, N2, channels), (2, 0, 1))
    turned = turned.reshape(toks, narrow, rows, N2)
    filt = half_filter(filter_spectrum, narrow)
    onward = [(i, i + 1) for i in range(segs - 1)]
    pieces = []
    for at in range(CHUNKS):
        span = slice(at * step, (at + 1) * step)
        x = lax.all_to_all(turned[:, span], "tok", 0, 0, tiled=True)
        main, tail = conv_call(x, filt[span], tables)
        carried = lax.ppermute(tail, "seg", onward)
        mixed = (main.astype(f32) + carried.astype(f32)).astype(jnp.bfloat16)
        pieces.append(lax.all_to_all(mixed, "tok", 0, 0, tiled=True))
    mixed = jnp.concatenate(pieces, axis=1).reshape(channels, rows, N2)
    mixed = jnp.transpose(mixed, (1, 2, 0)).reshape(tokens, channels)
    result = gate_out.astype(f32) * (mixed.astype(f32) + skip_gain[None, :] * gated.astype(f32))
    return result.astype(jnp.bfloat16)


def solution(mesh):
    return jax.shard_map(
        shards,
        mesh=mesh,
        in_specs=(
            P(("seg", "tok"), None),
            P(("seg", "tok"), None),
            P(("seg", "tok"), None),
            P(None, "tok", None, None),
            P(),
        ),
        out_specs=P(("seg", "tok"), None),
        check_vma=False,
    )
```

```python
import math

import jax
import jax.numpy as jnp
from jax import lax
from jax.experimental import pallas as pl
from jax.experimental.pallas import tpu as pltpu
from jax.sharding import PartitionSpec as P

N1 = 256
N2 = 512
HALF = N1 // 2
ROWS = HALF + 16
CHUNKS = 2
LINES = 16
GROUP = 4


def span_ids(count):
    return jnp.arange(count, dtype=jnp.int32)


def trig_tables(row_ids, col_ids, modulus):
    product = row_ids[:, None] * col_ids[None, :] % modulus
    angle = product.astype(jnp.float32) * jnp.float32(2.0 * math.pi / modulus)
    return (jnp.cos(angle), jnp.sin(angle))


def half_tables(base):
    rows = span_ids(ROWS)
    k1 = (base + rows) % N1
    used = rows <= HALF
    weight = jnp.where(used, jnp.where((rows == 0) | (rows == HALF), 1.0, 2.0), 0.0)
    weight = weight.astype(jnp.float32) / (N1 * N2)
    cos_one, sin_one = trig_tables(k1, span_ids(HALF), N1)
    forward = jnp.concatenate([cos_one, -sin_one], axis=0).astype(jnp.bfloat16)
    tw = jnp.stack(trig_tables(k1, span_ids(N2), N1 * N2))
    cos_two, sin_two = trig_tables(span_ids(N2), span_ids(N2), N2)
    cos_two = cos_two.astype(jnp.bfloat16)
    sin_two = sin_two.astype(jnp.bfloat16)
    there = jnp.block([[cos_two, -sin_two], [sin_two, cos_two]])
    back = jnp.block([[cos_two, sin_two], [-sin_two, cos_two]])
    inv_cos, inv_sin = trig_tables(span_ids(N1), k1, N1)
    inv_cos = inv_cos.astype(jnp.bfloat16).astype(jnp.float32) * weight[None, :]
    inv_sin = inv_sin.astype(jnp.bfloat16).astype(jnp.float32) * weight[None, :]
    inverse = jnp.concatenate([inv_cos, -inv_sin], axis=1).astype(jnp.bfloat16)
    return forward, tw, there, back, inverse


def turn_kernel(value_ref, gate_ref, *out_refs):
    f32 = jnp.float32
    gated = (value_ref[...].astype(f32) * gate_ref[...].astype(f32)).astype(jnp.bfloat16)
    lines = gated.shape[0] // N2
    turned = [gated[i * N2 : (i + 1) * N2].T for i in range(lines)]
    toks, step, _, _ = out_refs[0].shape
    turned = jnp.stack([t.astype(f32) for t in turned], axis=1).astype(jnp.bfloat16)
    turned = turned.reshape(toks, step * len(out_refs), lines, N2)
    for at, out_ref in enumerate(out_refs):
        out_ref[...] = turned[:, at * step : (at + 1) * step]


def turn_call(value, gate, toks):
    tokens, channels = value.shape
    rows = tokens // N2
    lines = min(rows, LINES)
    step = channels // toks // CHUNKS
    flat = pl.BlockSpec((lines * N2, channels), lambda i: (i, 0))
    out = jax.ShapeDtypeStruct((toks, step, rows, N2), jnp.bfloat16)
    return pl.pallas_call(
        turn_kernel,
        grid=(rows // lines,),
        in_specs=[flat, flat],
        out_specs=[pl.BlockSpec((toks, step, lines, N2), lambda i: (0, 0, i, 0))] * CHUNKS,
        out_shape=[out] * CHUNKS,
        compiler_params=pltpu.CompilerParams(vmem_limit_bytes=48 * 1024 * 1024),
        cost_estimate=pl.CostEstimate(
            flops=value.size, bytes_accessed=6 * value.size, transcendentals=0
        ),
    )(value, gate)


def finish_kernel(value_ref, gate_ref, gate_out_ref, skip_ref, *refs):
    f32 = jnp.float32
    out_ref = refs[-1]
    toks, step, lines, _ = refs[0].shape
    channels = out_ref.shape[1]
    mixed = jnp.concatenate([r[...] for r in refs[:-1]], axis=1).astype(f32)
    mixed = mixed.reshape(channels, lines, N2)
    for i in range(lines):
        span = slice(i * N2, (i + 1) * N2)
        line = mixed[:, i].astype(jnp.bfloat16).T.astype(f32)
        gated = value_ref[span].astype(f32) * gate_ref[span].astype(f32)
        gated = gated.astype(jnp.bfloat16).astype(f32)
        line = gate_out_ref[span].astype(f32) * (line + skip_ref[...] * gated)
        out_ref[span] = line.astype(jnp.bfloat16)


def finish_call(value, gate, gate_out, skip, pieces):
    tokens, channels = value.shape
    toks, step, rows, _ = pieces[0].shape
    lines = min(rows, LINES)
    flat = pl.BlockSpec((lines * N2, channels), lambda i: (i, 0))
    piece = pl.BlockSpec((toks, step, lines, N2), lambda i: (0, 0, i, 0))
    return pl.pallas_call(
        finish_kernel,
        grid=(rows // lines,),
        in_specs=[flat] * 3 + [pl.BlockSpec((1, channels), lambda i: (0, 0))] + [piece] * len(pieces),
        out_specs=flat,
        out_shape=jax.ShapeDtypeStruct(value.shape, jnp.bfloat16),
        compiler_params=pltpu.CompilerParams(vmem_limit_bytes=48 * 1024 * 1024),
        cost_estimate=pl.CostEstimate(
            flops=4 * value.size, bytes_accessed=10 * value.size, transcendentals=0
        ),
    )(value, gate, gate_out, skip[None, :], *pieces)


def conv_kernel(x_ref, h_ref, fwd_ref, tw_ref, there_ref, back_ref, inv_ref, main_ref, tail_ref):
    f32 = jnp.float32
    toks, count, rows, _ = x_ref.shape
    tc, ts = tw_ref[0], tw_ref[1]
    b = []
    for i in range(count):
        data = x_ref[:, i].astype(f32).reshape(HALF, N2).astype(jnp.bfloat16)
        a = jnp.dot(fwd_ref[...], data, preferred_element_type=f32)
        a_re, a_im = a[:ROWS], a[ROWS:]
        b_re = (a_re * tc + a_im * ts).astype(jnp.bfloat16)
        b_im = (a_im * tc - a_re * ts).astype(jnp.bfloat16)
        b.append(jnp.concatenate([b_re, b_im], axis=1))
    b = jnp.concatenate(b, axis=0)
    spec = jnp.dot(b, there_ref[...], preferred_element_type=f32)
    z = []
    for i in range(count):
        part = spec[i * ROWS : (i + 1) * ROWS]
        s_re, s_im = part[:, :N2], part[:, N2:]
        h_re = h_ref[i, 0].astype(f32)
        h_im = h_ref[i, 1].astype(f32)
        z_re = (s_re * h_re - s_im * h_im).astype(jnp.bfloat16)
        z_im = (s_re * h_im + s_im * h_re).astype(jnp.bfloat16)
        z.append(jnp.concatenate([z_re, z_im], axis=1))
    z = jnp.concatenate(z, axis=0)
    p = jnp.dot(z, back_ref[...], preferred_element_type=f32)
    for i in range(count):
        part = p[i * ROWS : (i + 1) * ROWS]
        p_re, p_im = part[:, :N2], part[:, N2:]
        q_re = (p_re * tc - p_im * ts).astype(jnp.bfloat16)
        q_im = (p_im * tc + p_re * ts).astype(jnp.bfloat16)
        q = jnp.concatenate([q_re, q_im], axis=0)
        conv = jnp.dot(inv_ref[...], q, preferred_element_type=f32)
        main_ref[:, i] = conv[:HALF].reshape(toks, rows, N2).astype(jnp.bfloat16)
        tail_ref[:, i] = conv[HALF:].reshape(toks, rows, N2).astype(jnp.bfloat16)


def conv_call(x, h, tables):
    parts, count, rows, _ = x.shape
    group = min(count, GROUP)
    block = pl.BlockSpec((parts, group, rows, N2), lambda c: (0, c, 0, 0))
    whole = lambda t: pl.BlockSpec(t.shape, lambda c: (0,) * t.ndim)
    out = jax.ShapeDtypeStruct(x.shape, jnp.bfloat16)
    flops = 4 * count * ROWS * N2 * (HALF + 2 * N2 + 2 * N2 + N1)
    return pl.pallas_call(
        conv_kernel,
        grid=(count // group,),
        in_specs=[block, pl.BlockSpec((group, 2, ROWS, N2), lambda c: (c, 0, 0, 0))]
        + [whole(t) for t in tables],
        out_specs=[block, block],
        out_shape=[out, out],
        compiler_params=pltpu.CompilerParams(vmem_limit_bytes=48 * 1024 * 1024),
        cost_estimate=pl.CostEstimate(
            flops=flops, bytes_accessed=6 * x.size + 2 * h.size, transcendentals=0
        ),
    )(x, h, *tables)


def half_filter(filt, narrow):
    toks, segs = lax.axis_size("tok"), lax.axis_size("seg")
    tok, seg = lax.axis_index("tok"), lax.axis_index("seg")
    rows = filt.shape[1]
    channels = filt.shape[3]
    share = rows // segs
    side = toks // 2
    upper = tok // side
    mine = lax.dynamic_slice(
        filt, (0, seg * share, 0, upper * (channels // 2)), (2, share, N2, channels // 2)
    )
    mine = jnp.transpose(mine, (3, 0, 1, 2)).reshape(side, narrow, 2, share, N2)
    own = tok % side
    parts = []
    for by in range(side):
        part = lax.dynamic_index_in_dim(mine, (own + side - by) % side, 0, keepdims=False)
        if by:
            pairs = [(t, t // side * side + (t + side - by) % side) for t in range(toks)]
            part = lax.ppermute(part, "tok", pairs)
        parts.append(part)
    mine = jnp.stack(parts)
    mine = jnp.take(mine, (span_ids(side) - own) % side, axis=0) if side > 2 else jnp.where(
        own == 0, mine, mine[::-1]
    )
    both = lax.all_gather(mine, "seg")
    both = jnp.transpose(both, (2, 3, 1, 0, 4, 5)).reshape(narrow, 2, HALF, N2)
    first = jnp.transpose(filt[:, 0], (2, 0, 1)).reshape(toks, narrow, 2, N2)
    last = jnp.zeros_like(first[0])
    for at in range(side):
        sent = jnp.where(tok == 0, first[side + at], first[at])
        last = last + lax.ppermute(sent, "tok", [(side, at), (0, side + at)])
    last = jnp.pad(last[:, :, None], ((0, 0), (0, 0), (0, ROWS - HALF - 1), (0, 0)))
    return jnp.concatenate([both, last], axis=2)


def shards(value, gate_in, gate_out, filter_spectrum, skip_gain):
    f32 = jnp.float32
    toks, segs = lax.axis_size("tok"), lax.axis_size("seg")
    narrow = value.shape[1] // toks
    step = narrow // CHUNKS
    base = lax.axis_index("tok") // (toks // 2) * HALF
    turned = turn_call(value, gate_in, toks)
    turned, filter_spectrum, base = lax.optimization_barrier((turned, filter_spectrum, base))
    tables = half_tables(base)
    filt = half_filter(filter_spectrum, narrow)
    onward = [(i, i + 1) for i in range(segs - 1)]
    pieces = []
    for at in range(CHUNKS):
        x = lax.all_to_all(turned[at], "tok", 0, 0, tiled=True)
        main, tail = conv_call(x, filt[at * step : (at + 1) * step], tables)
        carried = lax.ppermute(tail, "seg", onward)
        mixed = (main.astype(f32) + carried.astype(f32)).astype(jnp.bfloat16)
        pieces.append(lax.all_to_all(mixed, "tok", 0, 0, tiled=True))
    return finish_call(value, gate_in, gate_out, skip_gain, pieces)


def solution(mesh):
    return jax.shard_map(
        shards,
        mesh=mesh,
        in_specs=(
            P(("seg", "tok"), None),
            P(("seg", "tok"), None),
            P(("seg", "tok"), None),
            P(None, "tok", None, None),
            P(),
        ),
        out_specs=P(("seg", "tok"), None),
        check_vma=False,
    )
```

```python
import math

import jax
import jax.numpy as jnp
import numpy as np
from jax import lax
from jax.experimental import pallas as pl
from jax.experimental.pallas import tpu as pltpu
from jax.sharding import PartitionSpec as P

N1 = 256
N2 = 512
HALF = N1 // 2
ROWS = HALF + 16
CHUNKS = 2
LINES = 16
GROUP = 4


def trig_tables(row_ids, col_ids, modulus):
    product = row_ids[:, None] * col_ids[None, :] % modulus
    angle = product.astype(np.float32) * np.float32(2.0 * math.pi / modulus)
    return (np.cos(angle), np.sin(angle))


def rounded(table):
    return table.astype(jnp.bfloat16)


def row_tables(base, order):
    order = np.concatenate([order, np.zeros(ROWS - len(order), np.int32)])
    k1 = (base + order) % N1
    weight = np.where((order == 0) | (order == HALF), 1.0, 2.0)
    weight[HALF + 1 :] = 0.0
    weight = weight.astype(np.float32) / np.float32(N1 * N2)
    cos_one, sin_one = trig_tables(k1, np.arange(HALF, dtype=np.int32), N1)
    forward = rounded(np.concatenate([cos_one, -sin_one], axis=0))
    tw = np.stack(trig_tables(k1, np.arange(N2, dtype=np.int32), N1 * N2))
    inv = trig_tables(np.arange(N1, dtype=np.int32), k1, N1)
    inv_cos, inv_sin = [rounded(t).astype(np.float32) * weight[None, :] for t in inv]
    inverse = rounded(np.concatenate([inv_cos, -inv_sin], axis=1))
    return forward, tw, inverse


def half_tables(upper, order):
    halves = zip(row_tables(0, order), row_tables(HALF, order))
    forward, tw, inverse = [jnp.where(upper == 0, *pair) for pair in halves]
    cos_two, sin_two = trig_tables(*[np.arange(N2, dtype=np.int32)] * 2, N2)
    cos_two, sin_two = rounded(cos_two), rounded(sin_two)
    there = jnp.asarray(np.block([[cos_two, -sin_two], [sin_two, cos_two]]))
    back = jnp.asarray(np.block([[cos_two, sin_two], [-sin_two, cos_two]]))
    return forward, tw, there, back, inverse


def turn_kernel(value_ref, gate_ref, *out_refs):
    f32 = jnp.float32
    gated = (value_ref[...].astype(f32) * gate_ref[...].astype(f32)).astype(jnp.bfloat16)
    lines = gated.shape[0] // N2
    turned = [gated[i * N2 : (i + 1) * N2].T for i in range(lines)]
    toks, step, _, _ = out_refs[0].shape
    turned = jnp.stack([t.astype(f32) for t in turned], axis=1).astype(jnp.bfloat16)
    turned = turned.reshape(toks, step * len(out_refs), lines, N2)
    for at, out_ref in enumerate(out_refs):
        out_ref[...] = turned[:, at * step : (at + 1) * step]


def turn_call(value, gate, toks):
    tokens, channels = value.shape
    rows = tokens // N2
    lines = min(rows, LINES)
    step = channels // toks // CHUNKS
    flat = pl.BlockSpec((lines * N2, channels), lambda i: (i, 0))
    out = jax.ShapeDtypeStruct((toks, step, rows, N2), jnp.bfloat16)
    return pl.pallas_call(
        turn_kernel,
        grid=(rows // lines,),
        in_specs=[flat, flat],
        out_specs=[pl.BlockSpec((toks, step, lines, N2), lambda i: (0, 0, i, 0))] * CHUNKS,
        out_shape=[out] * CHUNKS,
        compiler_params=pltpu.CompilerParams(vmem_limit_bytes=48 * 1024 * 1024),
        cost_estimate=pl.CostEstimate(
            flops=value.size, bytes_accessed=6 * value.size, transcendentals=0
        ),
    )(value, gate)


def finish_kernel(value_ref, gate_ref, gate_out_ref, skip_ref, *refs):
    f32 = jnp.float32
    out_ref = refs[-1]
    toks, step, lines, _ = refs[0].shape
    channels = out_ref.shape[1]
    mixed = jnp.concatenate([r[...] for r in refs[:-1]], axis=1).astype(f32)
    mixed = mixed.reshape(channels, lines, N2)
    for i in range(lines):
        span = slice(i * N2, (i + 1) * N2)
        line = mixed[:, i].astype(jnp.bfloat16).T.astype(f32)
        gated = value_ref[span].astype(f32) * gate_ref[span].astype(f32)
        gated = gated.astype(jnp.bfloat16).astype(f32)
        line = gate_out_ref[span].astype(f32) * (line + skip_ref[...] * gated)
        out_ref[span] = line.astype(jnp.bfloat16)


def finish_call(value, gate, gate_out, skip, pieces):
    tokens, channels = value.shape
    toks, step, rows, _ = pieces[0].shape
    lines = min(rows, LINES)
    flat = pl.BlockSpec((lines * N2, channels), lambda i: (i, 0))
    piece = pl.BlockSpec((toks, step, lines, N2), lambda i: (0, 0, i, 0))
    return pl.pallas_call(
        finish_kernel,
        grid=(rows // lines,),
        in_specs=[flat] * 3 + [pl.BlockSpec((1, channels), lambda i: (0, 0))] + [piece] * len(pieces),
        out_specs=flat,
        out_shape=jax.ShapeDtypeStruct(value.shape, jnp.bfloat16),
        compiler_params=pltpu.CompilerParams(vmem_limit_bytes=48 * 1024 * 1024),
        cost_estimate=pl.CostEstimate(
            flops=4 * value.size, bytes_accessed=10 * value.size, transcendentals=0
        ),
    )(value, gate, gate_out, skip[None, :], *pieces)


def conv_kernel(x_ref, h_ref, last_ref, fwd_ref, tw_ref, there_ref, back_ref, inv_ref, main_ref, tail_ref):
    f32 = jnp.float32
    toks, count, rows, _ = x_ref.shape
    tc, ts = tw_ref[0], tw_ref[1]
    b = []
    for i in range(count):
        data = x_ref[:, i].astype(f32).reshape(HALF, N2).astype(jnp.bfloat16)
        a = jnp.dot(fwd_ref[...], data, preferred_element_type=f32)
        a_re, a_im = a[:ROWS], a[ROWS:]
        b_re = (a_re * tc + a_im * ts).astype(jnp.bfloat16)
        b_im = (a_im * tc - a_re * ts).astype(jnp.bfloat16)
        b.append(jnp.concatenate([b_re, b_im], axis=1))
    b = jnp.concatenate(b, axis=0)
    spec = jnp.dot(b, there_ref[...], preferred_element_type=f32)
    z = []
    for i in range(count):
        part = spec[i * ROWS : (i + 1) * ROWS]
        s_re, s_im = part[:, :N2], part[:, N2:]
        h = h_ref[:, :, i].astype(f32)
        share = h.shape[2] // 2
        last = last_ref[i].astype(f32)
        h_re = jnp.concatenate([h[:, :, :share].reshape(HALF, N2), last[:16]], axis=0)
        h_im = jnp.concatenate([h[:, :, share:].reshape(HALF, N2), last[16:]], axis=0)
        z_re = (s_re * h_re - s_im * h_im).astype(jnp.bfloat16)
        z_im = (s_re * h_im + s_im * h_re).astype(jnp.bfloat16)
        z.append(jnp.concatenate([z_re, z_im], axis=1))
    z = jnp.concatenate(z, axis=0)
    p = jnp.dot(z, back_ref[...], preferred_element_type=f32)
    for i in range(count):
        part = p[i * ROWS : (i + 1) * ROWS]
        p_re, p_im = part[:, :N2], part[:, N2:]
        q_re = (p_re * tc - p_im * ts).astype(jnp.bfloat16)
        q_im = (p_im * tc + p_re * ts).astype(jnp.bfloat16)
        q = jnp.concatenate([q_re, q_im], axis=0)
        conv = jnp.dot(inv_ref[...], q, preferred_element_type=f32)
        main_ref[:, i] = conv[:HALF].reshape(toks, rows, N2).astype(jnp.bfloat16)
        tail_ref[:, i] = conv[HALF:].reshape(toks, rows, N2).astype(jnp.bfloat16)


def conv_call(x, h, last, at, tables):
    parts, count, rows, _ = x.shape
    group = min(count, GROUP)
    first = at * (count // group)
    block = pl.BlockSpec((parts, group, rows, N2), lambda c: (0, c, 0, 0))
    whole = lambda t: pl.BlockSpec(t.shape, lambda c: (0,) * t.ndim)
    out = jax.ShapeDtypeStruct(x.shape, jnp.bfloat16)
    flops = 4 * count * ROWS * N2 * (HALF + 2 * N2 + 2 * N2 + N1)
    return pl.pallas_call(
        conv_kernel,
        grid=(count // group,),
        in_specs=[
            block,
            pl.BlockSpec(h.shape[:2] + (group,) + h.shape[3:], lambda c: (0, 0, c + first, 0, 0)),
            pl.BlockSpec((group,) + last.shape[1:], lambda c: (c + first, 0, 0)),
        ]
        + [whole(t) for t in tables],
        out_specs=[block, block],
        out_shape=[out, out],
        compiler_params=pltpu.CompilerParams(vmem_limit_bytes=48 * 1024 * 1024),
        cost_estimate=pl.CostEstimate(
            flops=flops, bytes_accessed=6 * x.size + 2 * h.size // CHUNKS, transcendentals=0
        ),
    )(x, h, last, *tables)


def half_filter(filt, narrow):
    toks, segs = lax.axis_size("tok"), lax.axis_size("seg")
    tok, seg = lax.axis_index("tok"), lax.axis_index("seg")
    rows, channels = filt.shape[1], filt.shape[3]
    share = rows // segs
    side = toks // 2
    upper = tok // side
    own = tok % side
    mine = lax.dynamic_slice(
        filt, (0, seg * share, 0, upper * (channels // 2)), (2, share, N2, channels // 2)
    )
    mine = jnp.transpose(mine, (3, 0, 1, 2)).reshape(side, narrow, 2 * share, N2)
    parts = []
    for by in range(side):
        part = lax.dynamic_index_in_dim(mine, (own + side - by) % side, 0, keepdims=False)
        if by:
            pairs = [(t, t // side * side + (t + side - by) % side) for t in range(toks)]
            part = lax.ppermute(part, "tok", pairs)
        parts.append(part)
    if side == 2:
        mine = jnp.where(own == 0, jnp.stack(parts), jnp.stack(parts[::-1]))
    else:
        mine = jnp.take(jnp.stack(parts), (jnp.arange(side) + side - own) % side, axis=0)
    both = lax.all_gather(mine, "seg")
    order = np.arange(HALF, dtype=np.int32)
    if share % 8:
        both = both.reshape(segs, side, narrow, 2, share, N2)
        both = jnp.transpose(both, (2, 3, 1, 0, 4, 5)).reshape(1, 1, narrow, 2 * HALF, N2)
    else:
        order = np.transpose(order.reshape(side, segs, share), (1, 0, 2)).reshape(HALF)
    order = np.append(order, np.int32(HALF))
    first = jnp.transpose(filt[:, 0], (2, 0, 1)).reshape(toks, narrow, 2, N2)
    last = jnp.zeros_like(first[0])
    for at in range(side):
        sent = jnp.where(tok == 0, first[side + at], first[at])
        last = last + lax.ppermute(sent, "tok", [(side, at), (0, side + at)])
    last = jnp.pad(last[:, :, None], ((0, 0), (0, 0), (0, 15), (0, 0)))
    return both, last.reshape(narrow, 32, N2), order


def shards(value, gate_in, gate_out, filter_spectrum, skip_gain):
    f32 = jnp.float32
    toks, segs = lax.axis_size("tok"), lax.axis_size("seg")
    narrow = value.shape[1] // toks
    turned = turn_call(value, gate_in, toks)
    both, last, order = half_filter(filter_spectrum, narrow)
    tables = half_tables(lax.axis_index("tok") // (toks // 2), order)
    onward = [(i, i + 1) for i in range(segs - 1)]
    pieces = []
    for at in range(CHUNKS):
        x = lax.all_to_all(turned[at], "tok", 0, 0, tiled=True)
        main, tail = conv_call(x, both, last, at, tables)
        carried = lax.ppermute(tail, "seg", onward)
        mixed = (main.astype(f32) + carried.astype(f32)).astype(jnp.bfloat16)
        pieces.append(lax.all_to_all(mixed, "tok", 0, 0, tiled=True))
    return finish_call(value, gate_in, gate_out, skip_gain, pieces)


def solution(mesh):
    return jax.shard_map(
        shards,
        mesh=mesh,
        in_specs=(
            P(("seg", "tok"), None),
            P(("seg", "tok"), None),
            P(("seg", "tok"), None),
            P(None, "tok", None, None),
            P(),
        ),
        out_specs=P(("seg", "tok"), None),
        check_vma=False,
    )
```
